32 devices in a mesh: section: 8 (over y, x, core), expert: 4 (over z).
Axes of the slice: x: 2, y: 2, z: 4, core: 2. Of those that a mesh axis runs over, the one named last changes fastest.
Arguments:
- resid: bfloat16 [384, 6144], P('expert', 'section'), may hold values from -6 to 6
- query: bfloat16 [384, 6144], P('section', 'expert'), may hold values from -300 to 300, as said below
- new_keys: bfloat16 [384, 1024], P('section', 'expert'), may hold values from -6 to 6
- new_values: bfloat16 [384, 1024], P('section', 'expert'), may hold values from -6 to 6
- cache_keys: bfloat16 [64, 1024, 1024], P('section', None, 'expert'), may hold values from -6 to 6
- cache_values: bfloat16 [64, 1024, 1024], P('section', None, 'expert'), may hold values from -6 to 6
- cache_len: int32 [64], P('section'), may hold values from 1 to 1024, as said below
- out_weight: bfloat16 [6144, 6144], P('expert', 'section'), may hold values from -0.078125 to 0.078125
- expert_ids: int32 [384, 2], replicated, may hold values from 0 to 3, all different within a row; in each aligned block of 96 rows (0 to 95, 96 to 191, ...) at most 60 rows name the same one
- gates: float32 [384, 2], P('expert'), may hold values from 0.05 to 0.95, as said below
- w_gate: bfloat16 [4, 6144, 8192], P('expert', None, 'section'), may hold values from -0.078125 to 0.078125
- w_up: bfloat16 [4, 6144, 8192], P('expert', None, 'section'), may hold values from -0.078125 to 0.078125
- w_down: bfloat16 [4, 8192, 6144], P('expert', 'section'), may hold values from -0.0625 to 0.0625
Outputs:
- layer_out: bfloat16 [384, 6144], P('expert', 'section')
The draws below stay inside these ranges and needn't reach their ends.
Inputs may be any that keep to these rules, and one draw needn't show every extreme that they name: `query`: some queries may be far larger than typical. `cache_len`: at least one request's cache holds all 1024 positions. `expert_ids`: each row names two different experts; in each aligned block of 96 rows no expert is named by more than 60 rows. `gates`: the two gate weights of a row are positive and sum to one.
All inputs are finite; a program needn't handle non-finite values.
Results may differ from the reference program's by a relative error of at most 0.0055.
Values may be sent and summed in bfloat16 or wider, within the bound.
No kernel may reach another device: no remote copies, remote signals or barrier semaphores. Data moves between devices by JAX's collectives and lax.ppermute only.
A program may use at most 128 MiB of HBM per device.

```python
import math
import jax
import jax.numpy as jnp
import numpy as np
from jax import lax

D = 6144
FF = 8192
HQ = 48
KV = 8
HD = 128
TOP = 2
DRAFT = 6
CACHE = 1024
EXPERTS = 4
REQ = 64
ROWS = 384
ROWS_BLK = 96
CAP = 60


def draw_query(key, part):
    key = jax.random.fold_in(key, 1)
    values = jnp.clip(jax.random.normal(key, (ROWS, HQ * HD), jnp.float32), -6.0, 6.0)
    return values.astype(jnp.bfloat16)


def draw_cache_len(key, part):
    key = jax.random.fold_in(key, 5)
    lengths = jax.random.randint(key, (REQ,), 1, CACHE + 1)
    longest = jax.random.randint(jax.random.fold_in(key, 6), (), 0, REQ)
    return lengths.at[longest].set(CACHE).astype(jnp.int32)


def draw_gates(key, part):
    key = jax.random.fold_in(key, 7)
    leading = jax.random.uniform(key, (ROWS,), jnp.float32, minval=0.5, maxval=0.95)
    return jnp.stack([leading, 1.0 - leading], axis=1).astype(jnp.float32)


def level_of(stream_key, extent, pieces, least, high):
    def one(axis_at, parts):
        steps = jax.random.uniform(jax.random.fold_in(jax.random.fold_in(stream_key, 6), axis_at), (parts,), jnp.float32, least / len(pieces), high / len(pieces))
        return jnp.repeat(jnp.exp(steps), extent[axis_at] // parts).reshape((-1,) + (1,) * (len(extent) - axis_at - 1))

    factor_of = one(*pieces[0])
    for cut in pieces[1:]:
        factor_of = factor_of * one(*cut)
    return factor_of


def shared_out(stream_key, own, number, rows, count, top, reach, skew):
    order = jax.random.permutation(stream_key, count)
    packed, ordinary = load_shares(count, rows * top, reach, skew, True), load_shares(count, rows * top, reach, skew, False)
    places = jnp.arange(count)

    def named(sizes, turn):
        used = int((sizes > 0).sum())
        fixed = max(1, used // 4)
        passed = fixed + (places - fixed + turn * (used - fixed)) % max(1, count - fixed)
        return jnp.zeros((count,), jnp.int32).at[order[jnp.where(places < fixed, places, passed)]].set(jnp.asarray(sizes, jnp.int32))

    sizes = jnp.where(number % 4 == 0, named(packed, number // 4), named(ordinary, number - number // 4 - 1))
    mixed = jax.random.permutation(jax.random.fold_in(own, 3), count)
    giver, sink = mixed[0:count // 2 * 2:2], mixed[1:count // 2 * 2:2]
    room = jnp.minimum(sizes[giver] - 1, reach - sizes[sink]) // 2
    room = jnp.where((giver == order[0]) | (sink == order[0]) | (sizes[sink] == 0), 0, jnp.maximum(room, 0))
    passed = jax.random.randint(jax.random.fold_in(own, 4), (count // 2,), 0, 1 << 20) % (room + 1)
    sizes = sizes.at[giver].add(-passed).at[sink].add(passed)
    items = jnp.searchsorted(jnp.cumsum(sizes), jnp.arange(rows * top), side="right").astype(jnp.int32)
    grid = items.reshape(top, rows).T
    grid = grid[jax.random.permutation(jax.random.fold_in(own, 1), rows)]
    turn = jax.random.randint(jax.random.fold_in(own, 2), (rows, 1), 0, top)
    return jnp.take_along_axis(grid, (jnp.arange(top)[None, :] + turn) % top, axis=1)


def load_shares(number_of, total, bound, slope, full):
    portions = [(1 << 20) // math.isqrt(rank ** slope) + 1 for rank in range(1, number_of + 1)]
    largest = bound if full else min(bound, max(-(-total // number_of), total * portions[0] // sum(portions)))
    least = 1 if total - largest >= number_of - 1 else 0
    counts, surplus = [largest] + [least] * (number_of - 1), total - largest - least * (number_of - 1)
    while surplus > 0:
        free = [i for i in range(1, number_of) if counts[i] < largest] or [i for i in range(1, number_of) if counts[i] < bound]
        mass, left = sum([portions[i] for i in free]), surplus
        for i in free:
            more = min(bound - counts[i], max(1, left * portions[i] // mass), surplus)
            counts[i] = counts[i] + more
            surplus = surplus - more
    return np.array(counts)


def scatter_about(rng, extent, spread, reach, split=(), held_as=jnp.bfloat16):
    array = spread * jax.random.normal(rng, extent, jnp.float32)
    if split:
        array = array * level_of(rng, extent, split, -0.22, 0.18)
    return jnp.clip(array, -reach, reach).astype(held_as)


def setup_inputs(seed: int = 0) -> dict:
    key_of = jax.random.split(jax.random.key(seed), 14)
    resid = scatter_about(key_of[0], (ROWS, D), 1.0, 6.0, ((0, 4), (1, 8)))
    query = draw_query(jax.random.fold_in(key_of[13], 71), 0)
    new_keys = scatter_about(key_of[2], (ROWS, KV * HD), 1.0, 6.0, ((0, 8), (1, 4)))
    new_values = scatter_about(key_of[3], (ROWS, KV * HD), 1.0, 6.0, ((0, 8), (1, 4)))
    cache_keys = scatter_about(key_of[4], (REQ, CACHE, KV * HD), 1.0, 6.0, ((0, 8), (2, 4)))
    cache_values = scatter_about(key_of[5], (REQ, CACHE, KV * HD), 1.0, 6.0, ((0, 8), (2, 4)))
    cache_len = draw_cache_len(jax.random.fold_in(key_of[13], 71), 0)
    out_weight = scatter_about(key_of[7], (HQ * HD, D), (HQ * HD) ** -0.5, 0.078125, ((0, 4), (1, 8)))
    expert_ids_keys = jax.random.split(jax.random.fold_in(key_of[8], 1), ROWS // ROWS_BLK)
    expert_ids_turns = jax.random.permutation(jax.random.fold_in(key_of[8], 3), ROWS // ROWS_BLK)
    expert_ids = jax.vmap(lambda own, number: shared_out(jax.random.fold_in(key_of[8], 2), own, number, ROWS_BLK, EXPERTS, TOP, CAP, 2))(expert_ids_keys, expert_ids_turns).reshape((ROWS, TOP))
    gates = draw_gates(jax.random.fold_in(key_of[13], 71), 0)
    w_gate = scatter_about(key_of[10], (EXPERTS, D, FF), D ** -0.5, 0.078125, ((0, 4), (2, 8)))
    w_up = scatter_about(key_of[11], (EXPERTS, D, FF), D ** -0.5, 0.078125, ((0, 4), (2, 8)))
    w_down = scatter_about(key_of[12], (EXPERTS, FF, D), FF ** -0.5, 0.0625, ((0, 4), (1, 8)))
    return dict(resid=resid, query=query, new_keys=new_keys, new_values=new_values, cache_keys=cache_keys, cache_values=cache_values, cache_len=cache_len, out_weight=out_weight, expert_ids=expert_ids, gates=gates, w_gate=w_gate, w_up=w_up, w_down=w_down)


def attend_request(operands):
    queries, draft_keys, draft_values, past_keys, past_values, length = operands
    groups = HQ // KV
    scale = 1.0 / math.sqrt(HD)
    qmat = queries.astype(jnp.float32).reshape(DRAFT, KV, groups, HD)
    past_k = past_keys.astype(jnp.float32).reshape(CACHE, KV, HD)
    past_v = past_values.astype(jnp.float32).reshape(CACHE, KV, HD)
    new_k = draft_keys.astype(jnp.float32).reshape(DRAFT, KV, HD)
    new_v = draft_values.astype(jnp.float32).reshape(DRAFT, KV, HD)
    past_scores = jnp.einsum('dkgh,ckh->kgdc', qmat, past_k) * scale
    valid = jnp.arange(CACHE, dtype=jnp.int32) < length
    past_scores = jnp.where(valid[None, None, None, :], past_scores, -1e+30)
    new_scores = jnp.einsum('dkgh,ekh->kgde', qmat, new_k) * scale
    causal = jnp.arange(DRAFT)[:, None] >= jnp.arange(DRAFT)[None, :]
    new_scores = jnp.where(causal[None, None], new_scores, -1e+30)
    top_score = jnp.maximum(lax.optimization_barrier(jnp.max(past_scores, axis=-1)), lax.optimization_barrier(jnp.max(new_scores, axis=-1)))
    past_exp = jnp.exp(past_scores - top_score[..., None])
    new_exp = jnp.exp(new_scores - top_score[..., None])
    total = lax.optimization_barrier(jnp.sum(past_exp, axis=-1)) + lax.optimization_barrier(jnp.sum(new_exp, axis=-1))
    past_prob = (past_exp / total[..., None]).astype(jnp.bfloat16).astype(jnp.float32)
    new_prob = (new_exp / total[..., None]).astype(jnp.bfloat16).astype(jnp.float32)
    mixed = jnp.einsum('kgdc,ckh->dkgh', past_prob, past_v) + jnp.einsum('kgde,ekh->dkgh', new_prob, new_v)
    return mixed.reshape(DRAFT, HQ * HD).astype(jnp.bfloat16)

def run_expert(operands):
    buffer, gate_w, up_w, down_w = operands
    gate_acc = jnp.dot(buffer, gate_w, preferred_element_type=jnp.float32)
    up_acc = jnp.dot(buffer, up_w, preferred_element_type=jnp.float32)
    activated = (jax.nn.silu(gate_acc) * up_acc).astype(jnp.bfloat16)
    return jnp.dot(activated, down_w, preferred_element_type=jnp.float32)

def reference(resid, query, new_keys, new_values, cache_keys, cache_values, cache_len, out_weight, expert_ids, gates, w_gate, w_up, w_down):
    attended = lax.map(attend_request, (query.reshape(REQ, DRAFT, HQ * HD), new_keys.reshape(REQ, DRAFT, KV * HD), new_values.reshape(REQ, DRAFT, KV * HD), cache_keys, cache_values, cache_len))
    attended = attended.reshape(ROWS, HQ * HD)
    projected = jnp.dot(attended, out_weight, preferred_element_type=jnp.float32)
    hidden_in = (resid.astype(jnp.float32) + projected).astype(jnp.bfloat16)
    blocks = EXPERTS
    flat = expert_ids.reshape(blocks, ROWS_BLK * TOP)
    onehot = (flat[..., None] == jnp.arange(EXPERTS, dtype=jnp.int32)).astype(jnp.int32)
    slot = lax.optimization_barrier(jnp.sum((jnp.cumsum(onehot, axis=1) - onehot) * onehot, axis=-1))
    block_idx = jnp.arange(blocks, dtype=jnp.int32)[:, None]
    position = (flat * (blocks * CAP) + block_idx * CAP + slot).reshape(ROWS, TOP).astype(jnp.int32)
    row_idx = jnp.broadcast_to(jnp.arange(ROWS, dtype=jnp.int32)[:, None], (ROWS, TOP))
    buffer_rows = jnp.full((EXPERTS * blocks * CAP,), ROWS, jnp.int32).at[position.reshape(-1)].set(row_idx.reshape(-1))
    padded = jnp.concatenate([hidden_in, jnp.zeros((1, D), jnp.bfloat16)], axis=0)
    buffers = padded[buffer_rows].reshape(EXPERTS, blocks * CAP, D)
    outputs = lax.map(run_expert, (buffers, w_gate, w_up, w_down)).reshape(EXPERTS * blocks * CAP, D)
    picked = outputs[position]
    mixture = lax.optimization_barrier(jnp.sum(gates[..., None] * picked, axis=1))
    return (hidden_in.astype(jnp.float32) + mixture).astype(jnp.bfloat16)
```

```python
import functools
import math

import jax
import jax.numpy as jnp
from jax import lax
from jax.experimental import pallas as pl
from jax.experimental.pallas import tpu as pltpu
from jax.sharding import PartitionSpec as P

HQ = 48
KV = 8
HD = 128
TOP = 2
GROUPS = HQ // KV
SCALE = 1.0 / math.sqrt(HD)
MASKED = -1e30
NT = (((1,), (1,)), ((), ()))


def spread(rows, drafts, transposed):
    shape = (rows, rows // drafts * 8) if transposed else (rows // drafts * 8, rows)
    at = lax.broadcasted_iota(jnp.int32, shape, 1 if transposed else 0)
    row = lax.broadcasted_iota(jnp.int32, shape, 0 if transposed else 1)
    inside = at & 7
    return ((inside < drafts) & ((at >> 3) * drafts + inside == row)).astype(jnp.bfloat16)


def attend_kernel(
    drafts, len_hbm, q_hbm, nk_hbm, nv_hbm, ck_hbm, cv_hbm, w_hbm, o_ref, w_ref, *scratch
):
    len_ref, q_ref, nk_ref, nv_ref, ck_ref, cv_ref, qs, scores, acc, sem, k_sem, v_sem, w_sem = scratch
    requests, size, width = ck_ref.shape
    rows = q_ref.shape[0]
    heads = width // HD
    group = GROUPS * 8
    wide = heads * group

    small = [
        pltpu.make_async_copy(src, dst, sem.at[i])
        for i, (src, dst) in enumerate(
            ((q_hbm, q_ref), (len_hbm, len_ref), (nk_hbm, nk_ref), (nv_hbm, nv_ref))
        )
    ]
    keys = [pltpu.make_async_copy(ck_hbm.at[r], ck_ref.at[r], k_sem.at[r]) for r in range(requests)]
    values = [
        pltpu.make_async_copy(cv_hbm.at[r], cv_ref.at[r], v_sem.at[r]) for r in range(requests)
    ]
    part = w_ref.shape[0] // 4
    weights = [
        pltpu.make_async_copy(
            w_hbm.at[i * part : (i + 1) * part], w_ref.at[i * part : (i + 1) * part], w_sem.at[i]
        )
        for i in range(4)
    ]
    for copy in small:
        copy.start()
    for pair in zip(keys, values):
        for copy in pair:
            copy.start()
    for copy in weights:
        copy.start()
    for copy in small:
        copy.wait()
    qs[...] = dot(spread(rows, drafts, False), q_ref[...])

    at = lax.broadcasted_iota(jnp.int32, (wide, rows), 1)
    draft_at = lax.broadcasted_iota(jnp.int32, (wide, rows), 0) & 7
    past_at = lax.broadcasted_iota(jnp.int32, (wide, size), 1)

    def queries(r):
        q_all = qs[r * 8 : (r + 1) * 8, :]
        zero = jnp.zeros((group, HD), jnp.float32)
        parts = []
        for h in range(heads):
            q = jnp.concatenate(
                [
                    q_all[:, (h * GROUPS + g) * HD : (h * GROUPS + g + 1) * HD]
                    for g in range(GROUPS)
                ],
                axis=0,
            )
            parts.append(jnp.concatenate([q if j == h else zero for j in range(heads)], axis=1))
        return jnp.concatenate(parts, axis=0).astype(jnp.bfloat16)

    def score(r):
        past = lax.dot_general(queries(r), ck_ref[r], NT, preferred_element_type=jnp.float32)
        scores[r % 4] = jnp.where(past_at < len_ref[r], past * SCALE, MASKED)

    def mix(r):
        past = scores[r % 4]
        new = lax.dot_general(queries(r), nk_ref[...], NT, preferred_element_type=jnp.float32)
        key_at = at - r * drafts
        new_ok = (key_at >= 0) & (key_at <= draft_at) & (key_at < drafts)
        new = jnp.where(new_ok, new * SCALE, MASKED)
        top = jnp.maximum(
            jnp.max(past, axis=1, keepdims=True), jnp.max(new, axis=1, keepdims=True)
        )
        past = jnp.exp(past - top)
        new = jnp.exp(new - top)
        total = jnp.sum(past, axis=1, keepdims=True) + jnp.sum(new, axis=1, keepdims=True)
        inverse = 1.0 / total
        mixed = dot((past * inverse).astype(jnp.bfloat16), cv_ref[r])
        mixed = mixed + dot((new * inverse).astype(jnp.bfloat16), nv_ref[...])
        for h in range(heads):
            for g in range(GROUPS):
                col = (h * GROUPS + g) * HD
                row = h * group + g * 8
                acc[r * 8 : (r + 1) * 8, col : col + HD] = mixed[
                    row : row + 8, h * HD : (h + 1) * HD
                ]

    pairs = [range(i, min(i + 2, requests)) for i in range(0, requests, 2)]
    for r in pairs[0]:
        keys[r].wait()
    for r in pairs[0]:
        score(r)
    for i, pair in enumerate(pairs):
        following = pairs[i + 1] if i + 1 < len(pairs) else ()
        for r in following:
            keys[r].wait()
        for r in pair:
            values[r].wait()
        for r in following:
            score(r)
        for r in pair:
            mix(r)
    kept = spread(rows, drafts, True)
    o_ref[...] = dot(kept, acc[...].astype(jnp.bfloat16)).astype(jnp.bfloat16)
    for copy in weights:
        copy.wait()


def attend(query, new_keys, new_values, cache_keys, cache_values, cache_len, weight):
    requests, size, width = cache_keys.shape
    rows, q_width = query.shape
    wide = width // HD * GROUPS * 8
    f32, bf16 = jnp.float32, jnp.bfloat16
    operands = [
        pltpu.with_memory_space_constraint(v, pltpu.HBM)
        for v in (cache_len, query, new_keys, new_values, cache_keys, cache_values, weight)
    ]
    return pl.pallas_call(
        functools.partial(attend_kernel, rows // requests),
        in_specs=[pl.BlockSpec(memory_space=pl.ANY)] * len(operands),
        out_specs=[pl.BlockSpec(memory_space=pltpu.VMEM)] * 2,
        out_shape=[
            jax.ShapeDtypeStruct(query.shape, bf16),
            pltpu.VMEM(weight.shape, weight.dtype),
        ],
        scratch_shapes=[
            pltpu.SMEM(cache_len.shape, jnp.int32),
            pltpu.VMEM(query.shape, bf16),
            pltpu.VMEM(new_keys.shape, bf16),
            pltpu.VMEM(new_values.shape, bf16),
            pltpu.VMEM(cache_keys.shape, bf16),
            pltpu.VMEM(cache_values.shape, bf16),
            pltpu.VMEM((requests * 8, q_width), f32),
            pltpu.VMEM((4, wide, size), f32),
            pltpu.VMEM((requests * 8, q_width), f32),
            pltpu.SemaphoreType.DMA((4,)),
            pltpu.SemaphoreType.DMA((requests,)),
            pltpu.SemaphoreType.DMA((requests,)),
            pltpu.SemaphoreType.DMA((4,)),
        ],
        compiler_params=pltpu.CompilerParams(vmem_limit_bytes=20 * 1024 * 1024),
        cost_estimate=pl.CostEstimate(
            flops=4 * rows * size * q_width,
            bytes_accessed=4 * requests * size * width,
            transcendentals=rows * size * q_width // HD,
        ),
        name="attend",
    )(*operands)


def project_kernel(at_ref, *refs):
    pieces, (w_ref, own_ref, *out_refs, scratch) = refs[: at_ref.shape[0]], refs[at_ref.shape[0] :]
    part = pieces[0].shape[0]
    rows = own_ref.shape[0]
    for i, piece in enumerate(pieces):
        scratch[pl.ds(pl.multiple_of(at_ref[i] * part, 16), part), :] = piece[...]
    product = dot(scratch[...], w_ref[...])
    own_ref[...] = product[:rows, :]
    for i, out in enumerate(out_refs):
        out[...] = product[(i + 1) * rows : (i + 2) * rows, :].astype(out.dtype)


def project(places, pieces, weight, blocks):
    part, depth = pieces[0].shape
    width = weight.shape[1]
    rows = part * len(pieces) // blocks
    vmem = pl.BlockSpec(memory_space=pltpu.VMEM)
    own = jax.ShapeDtypeStruct((rows, width), jnp.float32)
    sent = jax.ShapeDtypeStruct((rows, width), jnp.bfloat16)
    return pl.pallas_call(
        project_kernel,
        in_specs=[pl.BlockSpec(memory_space=pltpu.SMEM)] + [vmem] * (len(pieces) + 1),
        out_specs=[vmem] * blocks,
        out_shape=[own] + [sent] * (blocks - 1),
        scratch_shapes=[pltpu.VMEM((part * len(pieces), depth), jnp.bfloat16)],
        compiler_params=pltpu.CompilerParams(vmem_limit_bytes=8 * 1024 * 1024),
        cost_estimate=pl.CostEstimate(
            flops=2 * part * len(pieces) * depth * width,
            bytes_accessed=2 * depth * width,
            transcendentals=0,
        ),
        name="project",
    )(places, *pieces, weight)


def fetch_kernel(dim, count, at_ref, src, *refs):
    parts, sem = refs[-1 - count : -1], refs[-1]
    width = parts[0].shape[dim] // 2
    copies = []
    for i, part in enumerate(parts):
        for side in range(2):
            n = 2 * i + side
            start = pl.multiple_of(at_ref[n] * width, 128)
            here = slice(side * width, (side + 1) * width)
            if dim == 0:
                pair = src.at[0, pl.ds(start, width), :], part.at[here, :]
            else:
                pair = src.at[0, :, pl.ds(start, width)], part.at[:, here]
            copies.append(pltpu.make_async_copy(*pair, sem.at[n]))
    for copy in copies:
        copy.start()
    for copy in copies:
        copy.wait()


def fetch(weight, dim, at, *after):
    count = at.shape[0] // 2
    shape = list(weight.shape[1:])
    shape[dim] //= count
    weight = pltpu.with_memory_space_constraint(weight, pltpu.HBM)
    return pl.pallas_call(
        functools.partial(fetch_kernel, dim, count),
        in_specs=[pl.BlockSpec(memory_space=pltpu.SMEM)]
        + [pl.BlockSpec(memory_space=pl.ANY)] * (1 + len(after)),
        out_specs=[pl.BlockSpec(memory_space=pltpu.VMEM)] * count,
        out_shape=[pltpu.VMEM(tuple(shape), weight.dtype)] * count,
        scratch_shapes=[pltpu.SemaphoreType.DMA((2 * count,))],
        compiler_params=pltpu.CompilerParams(vmem_limit_bytes=1024 * 1024),
        cost_estimate=pl.CostEstimate(
            flops=0, bytes_accessed=2 * math.prod(weight.shape), transcendentals=0
        ),
        name="fetch",
    )(at, weight, *after)


def swap(value, axis, mask):
    size = lax.axis_size(axis)
    return lax.ppermute(value, axis, [(i, i ^ mask) for i in range(size)])


def dot(a, b):
    return jnp.dot(a, b, preferred_element_type=jnp.float32)


def share(value):
    chips = lax.axis_size("section") // 2
    return [value] + [swap(value, "section", 2 * k) for k in range(1, chips)]


def exchange(parts):
    count = lax.axis_size("expert")
    arrived = {k: swap(parts[k], "expert", k) for k in reversed(range(1, count))}
    return [arrived[k] for k in range(1, count)]


def per_device(
    resid,
    query,
    new_keys,
    new_values,
    cache_keys,
    cache_values,
    cache_len,
    out_weight,
    expert_ids,
    gates,
    w_gate,
    w_up,
    w_down,
):
    f32, bf16 = jnp.float32, jnp.bfloat16
    sections = lax.axis_size("section")
    experts = lax.axis_size("expert")
    chips = sections // 2
    section = lax.axis_index("section")
    own = lax.axis_index("expert")
    chip, core = section // 2, section % 2
    block_rows, width = resid.shape
    capacity = (block_rows * TOP * 5 + 4 * experts - 1) // (4 * experts)
    slots = -(-capacity // 16) * 16

    ids = lax.dynamic_slice_in_dim(expert_ids, own * block_rows, block_rows, 0)
    relative = ids ^ own
    order = jnp.arange(experts, dtype=jnp.int32)
    names = relative[:, :, None] == order
    named = jnp.any(names, axis=1)
    row = jnp.arange(block_rows, dtype=jnp.int32)
    earlier = (row[None, :] < row[:, None]).astype(bf16)
    rank = dot(earlier, named.astype(bf16)).astype(jnp.int32)
    slot = jnp.arange(slots, dtype=jnp.int32)
    hit = rank[:, :, None] == slot
    pick = (hit & named[:, :, None]).astype(bf16).reshape(block_rows, experts * slots)
    place = [
        (hit & names[:, k, :, None]).astype(bf16).reshape(block_rows, experts * slots)
        for k in range(TOP)
    ]

    attended, out_weight = attend(
        query, new_keys, new_values, cache_keys, cache_values, cache_len, out_weight
    )
    same = [attended] + [swap(attended, "section", 2 * k) for k in range(1, chips)]
    step = jnp.arange(2 * chips, dtype=jnp.int32)
    found = section ^ step
    block = (step % chips) ^ chip ^ own
    places = block * 2 + (core ^ (step // chips))
    found, places = lax.optimization_barrier((found, places))
    same, gate_parts = lax.optimization_barrier((same, fetch(w_gate, 0, found, attended)))
    other = [swap(v, "section", 1) for v in same]
    projected = list(project(places, same + other, out_weight, experts))
    arrived = exchange(projected)
    hidden, up_parts = lax.optimization_barrier(
        (resid.astype(f32) + projected[0], fetch(w_up, 0, found, projected[0]))
    )
    for part in arrived:
        hidden = hidden + part.astype(f32)
    hidden_in = hidden.astype(bf16)

    buffers = lax.dot_general(
        pick, hidden_in, (((0,), (0,)), ((), ())), preferred_element_type=f32
    ).astype(bf16)
    buffers = buffers.reshape(experts, slots, width)
    early = [k for k in range(1, chips) if k & 2]
    first = {k: swap(buffers[0], "section", 2 * k) for k in early}
    rest = jnp.concatenate(exchange(buffers), axis=0)
    rest, first = lax.optimization_barrier((rest, first))
    received = jnp.concatenate([buffers[0], rest], axis=0)
    second = {k: swap(rest if k in first else received, "section", 2 * k) for k in range(1, chips)}

    sums = []
    for k in range(chips):
        if not k:
            same = received
        elif k in first:
            first[k], second[k], sums = lax.optimization_barrier((first[k], second[k], sums))
            same = jnp.concatenate([first[k], second[k]], axis=0)
        elif k == 1:
            down_parts = fetch(w_down, 1, found, *sums)
            same, sums, down_parts = lax.optimization_barrier((second[k], sums, down_parts))
        else:
            same, sums = lax.optimization_barrier((second[k], sums))
        for side, piece in enumerate((same, swap(same, "section", 1))):
            here = slice(side * width, (side + 1) * width)
            parts = [dot(piece, w[k][here]) for w in (gate_parts, up_parts)]
            sums = [a + b for a, b in zip(sums, parts)] if sums else parts
    gate_acc, up_acc = sums
    activated = (jax.nn.silu(gate_acc) * up_acc).astype(bf16)

    def down(k, side):
        here = slice(side * width, (side + 1) * width)
        return dot(activated, down_parts[k][:, here])

    order = sorted(range(1, chips), key=lambda k: (-(k & 2), -k))
    ahead = {k: down(k, 1).astype(bf16) for k in early}
    later, rest = {}, {}
    for k in order:
        for_core = ahead[k] if k in ahead else down(k, 1).astype(bf16)
        both = (down(k, 0) + swap(for_core, "section", 1).astype(f32)).astype(bf16)
        later[k], rest[k] = both[:slots], both[slots:]
        if k in ahead:
            later[k], rest[k], activated = lax.optimization_barrier((later[k], rest[k], activated))
    rest = {k: swap(rest[k], "section", 2 * k) for k in order}
    total = down(0, 0) + swap(down(0, 1).astype(bf16), "section", 1).astype(f32)
    mine, total = total[:slots], total[slots:]
    for k in order:
        total = total + rest[k].astype(f32)
    total, later = lax.optimization_barrier((total.astype(bf16), later))

    arrived = exchange([None] + jnp.split(total, experts - 1, axis=0))
    later = [swap(later[k], "section", 2 * k) for k in order]
    mine, arrived = lax.optimization_barrier((mine, arrived))
    for part in later:
        mine = mine + part.astype(f32)
    returned = jnp.concatenate([mine.astype(bf16)] + arrived, axis=0)
    mixture = sum(gates[:, k : k + 1] * dot(place[k], returned) for k in range(TOP))
    return (hidden_in.astype(f32) + mixture).astype(bf16)


def solution(mesh):
    in_specs = (
        P("expert", "section"),
        P("section", "expert"),
        P("section", "expert"),
        P("section", "expert"),
        P("section", None, "expert"),
        P("section", None, "expert"),
        P("section"),
        P("expert", "section"),
        P(),
        P("expert", None),
        P("expert", None, "section"),
        P("expert", None, "section"),
        P("expert", "section", None),
    )
    out_specs = P("expert", "section")
    return jax.shard_map(
        per_device, mesh=mesh, in_specs=in_specs, out_specs=out_specs, check_vma=False
    )
```

```python
import functools
import math

import jax
import jax.numpy as jnp
from jax import lax
from jax.experimental import pallas as pl
from jax.experimental.pallas import tpu as pltpu
from jax.sharding import PartitionSpec as P

HQ = 48
KV = 8
HD = 128
TOP = 2
GROUPS = HQ // KV
SCALE = 1.0 / math.sqrt(HD)
MASKED = -1e30
NT = (((1,), (1,)), ((), ()))


def spread(rows, drafts, transposed):
    shape = (rows, rows // drafts * 8) if transposed else (rows // drafts * 8, rows)
    at = lax.broadcasted_iota(jnp.int32, shape, 1 if transposed else 0)
    row = lax.broadcasted_iota(jnp.int32, shape, 0 if transposed else 1)
    inside = at & 7
    return ((inside < drafts) & ((at >> 3) * drafts + inside == row)).astype(jnp.bfloat16)


def attend_kernel(
    drafts, len_hbm, q_hbm, nk_hbm, nv_hbm, ck_hbm, cv_hbm, w_hbm, o_ref, w_ref, *scratch
):
    len_ref, q_ref, nk_ref, nv_ref, ck_ref, cv_ref, *scratch = scratch
    qs, spread_q, scores, new_scores, new_probs, mixed, inverse, acc, *scratch = scratch
    sem, k_sem, v_sem, w_sem = scratch
    requests, size, width = ck_ref.shape
    rows = q_ref.shape[0]
    heads = width // HD
    group = GROUPS * 8
    wide = heads * group

    small = [
        pltpu.make_async_copy(src, dst, sem.at[i])
        for i, (src, dst) in enumerate(
            ((q_hbm, q_ref), (len_hbm, len_ref), (nk_hbm, nk_ref), (nv_hbm, nv_ref))
        )
    ]
    keys = [pltpu.make_async_copy(ck_hbm.at[r], ck_ref.at[r], k_sem.at[r]) for r in range(requests)]
    values = [
        pltpu.make_async_copy(cv_hbm.at[r], cv_ref.at[r], v_sem.at[r]) for r in range(requests)
    ]
    part = w_ref.shape[0] // 4
    weights = [
        pltpu.make_async_copy(
            w_hbm.at[i * part : (i + 1) * part], w_ref.at[i * part : (i + 1) * part], w_sem.at[i]
        )
        for i in range(4)
    ]
    for copy in small:
        copy.start()
    for pair in zip(keys, values):
        for copy in pair:
            copy.start()
    for copy in weights:
        copy.start()
    for copy in small:
        copy.wait()
    qs[...] = dot(spread(rows, drafts, False), q_ref[...])

    place = lax.broadcasted_iota(jnp.int32, (1, size), 1)
    for r in range(requests):
        q_all = qs[r * 8 : (r + 1) * 8, :]
        zero = jnp.zeros((group, HD), jnp.float32)
        parts = []
        for h in range(heads):
            q = jnp.concatenate(
                [
                    q_all[:, (h * GROUPS + g) * HD : (h * GROUPS + g + 1) * HD]
                    for g in range(GROUPS)
                ],
                axis=0,
            )
            parts.append(jnp.concatenate([q if j == h else zero for j in range(heads)], axis=1))
        spread_q[r * wide : (r + 1) * wide, :] = jnp.concatenate(parts, axis=0).astype(jnp.bfloat16)
    new_scores[...] = lax.dot_general(
        spread_q[...], nk_ref[...], NT, preferred_element_type=jnp.float32
    )
    at = lax.broadcasted_iota(jnp.int32, (wide, rows), 1)
    draft_at = lax.broadcasted_iota(jnp.int32, (wide, rows), 0) & 7

    def score(r):
        here = slice(r * wide, (r + 1) * wide)
        past = lax.dot_general(spread_q[here, :], ck_ref[r], NT, preferred_element_type=jnp.float32)
        scores[r % 4] = past * SCALE + jnp.where(place < len_ref[r], 0.0, MASKED)

    def mix(r):
        here = slice(r * wide, (r + 1) * wide)
        past = scores[r % 4]
        key_at = at - r * drafts
        new_ok = (key_at >= 0) & (key_at <= draft_at) & (key_at < drafts)
        new = jnp.where(new_ok, new_scores[here, :] * SCALE, MASKED)
        top = jnp.maximum(
            jnp.max(past, axis=1, keepdims=True), jnp.max(new, axis=1, keepdims=True)
        )
        past = jnp.exp(past - top)
        new = jnp.exp(new - top)
        total = jnp.sum(past, axis=1, keepdims=True) + jnp.sum(new, axis=1, keepdims=True)
        inverse[here, :] = jnp.broadcast_to(1.0 / total, (wide, HD))
        new_probs[here, :] = new.astype(jnp.bfloat16)
        mixed[here, :] = dot(past.astype(jnp.bfloat16), cv_ref[r])

    pairs = [range(i, min(i + 2, requests)) for i in range(0, requests, 2)]
    for r in pairs[0]:
        keys[r].wait()
    for r in pairs[0]:
        score(r)
    for i, pair in enumerate(pairs):
        following = pairs[i + 1] if i + 1 < len(pairs) else ()
        for r in following:
            keys[r].wait()
        for r in pair:
            values[r].wait()
        for r in following:
            score(r)
        for r in pair:
            mix(r)
    mixed[...] = mixed[...] + dot(new_probs[...], nv_ref[...])
    for r in range(requests):
        for h in range(heads):
            for g in range(GROUPS):
                col = (h * GROUPS + g) * HD
                row = slice(r * wide + h * group + g * 8, r * wide + h * group + (g + 1) * 8)
                acc[r * 8 : (r + 1) * 8, col : col + HD] = (
                    mixed[row, h * HD : (h + 1) * HD] * inverse[row, :]
                )
    kept = spread(rows, drafts, True)
    o_ref[...] = dot(kept, acc[...].astype(jnp.bfloat16)).astype(jnp.bfloat16)
    for copy in weights:
        copy.wait()


def attend(query, new_keys, new_values, cache_keys, cache_values, cache_len, weight):
    requests, size, width = cache_keys.shape
    rows, q_width = query.shape
    wide = width // HD * GROUPS * 8
    f32, bf16 = jnp.float32, jnp.bfloat16
    operands = [
        pltpu.with_memory_space_constraint(v, pltpu.HBM)
        for v in (cache_len, query, new_keys, new_values, cache_keys, cache_values, weight)
    ]
    return pl.pallas_call(
        functools.partial(attend_kernel, rows // requests),
        in_specs=[pl.BlockSpec(memory_space=pl.ANY)] * len(operands),
        out_specs=[pl.BlockSpec(memory_space=pltpu.VMEM)] * 2,
        out_shape=[
            jax.ShapeDtypeStruct(query.shape, bf16),
            pltpu.VMEM(weight.shape, weight.dtype),
        ],
        scratch_shapes=[
            pltpu.SMEM(cache_len.shape, jnp.int32),
            pltpu.VMEM(query.shape, bf16),
            pltpu.VMEM(new_keys.shape, bf16),
            pltpu.VMEM(new_values.shape, bf16),
            pltpu.VMEM(cache_keys.shape, bf16),
            pltpu.VMEM(cache_values.shape, bf16),
            pltpu.VMEM((requests * 8, q_width), f32),
            pltpu.VMEM((requests * wide, width), bf16),
            pltpu.VMEM((4, wide, size), f32),
            pltpu.VMEM((requests * wide, rows), f32),
            pltpu.VMEM((requests * wide, rows), bf16),
            pltpu.VMEM((requests * wide, width), f32),
            pltpu.VMEM((requests * wide, HD), f32),
            pltpu.VMEM((requests * 8, q_width), f32),
            pltpu.SemaphoreType.DMA((4,)),
            pltpu.SemaphoreType.DMA((requests,)),
            pltpu.SemaphoreType.DMA((requests,)),
            pltpu.SemaphoreType.DMA((4,)),
        ],
        compiler_params=pltpu.CompilerParams(vmem_limit_bytes=20 * 1024 * 1024),
        cost_estimate=pl.CostEstimate(
            flops=4 * rows * size * q_width,
            bytes_accessed=4 * requests * size * width,
            transcendentals=rows * size * q_width // HD,
        ),
        name="attend",
    )(*operands)


def project_kernel(at_ref, *refs):
    pieces, (w_ref, own_ref, *out_refs, scratch) = refs[: at_ref.shape[0]], refs[at_ref.shape[0] :]
    part = pieces[0].shape[0]
    rows = own_ref.shape[0]
    for i, piece in enumerate(pieces):
        scratch[pl.ds(pl.multiple_of(at_ref[i] * part, 16), part), :] = piece[...]
    product = dot(scratch[...], w_ref[...])
    own_ref[...] = product[:rows, :]
    for i, out in enumerate(out_refs):
        out[...] = product[(i + 1) * rows : (i + 2) * rows, :].astype(out.dtype)


def project(places, pieces, weight, blocks):
    part, depth = pieces[0].shape
    width = weight.shape[1]
    rows = part * len(pieces) // blocks
    vmem = pl.BlockSpec(memory_space=pltpu.VMEM)
    own = jax.ShapeDtypeStruct((rows, width), jnp.float32)
    sent = jax.ShapeDtypeStruct((rows, width), jnp.bfloat16)
    return pl.pallas_call(
        project_kernel,
        in_specs=[pl.BlockSpec(memory_space=pltpu.SMEM)] + [vmem] * (len(pieces) + 1),
        out_specs=[vmem] * blocks,
        out_shape=[own] + [sent] * (blocks - 1),
        scratch_shapes=[pltpu.VMEM((part * len(pieces), depth), jnp.bfloat16)],
        compiler_params=pltpu.CompilerParams(vmem_limit_bytes=8 * 1024 * 1024),
        cost_estimate=pl.CostEstimate(
            flops=2 * part * len(pieces) * depth * width,
            bytes_accessed=2 * depth * width,
            transcendentals=0,
        ),
        name="project",
    )(places, *pieces, weight)


def fetch_kernel(dim, count, at_ref, src, *refs):
    parts, sem = refs[-1 - count : -1], refs[-1]
    width = parts[0].shape[dim] // 2
    copies = []
    for i, part in enumerate(parts):
        for side in range(2):
            n = 2 * i + side
            start = pl.multiple_of(at_ref[n] * width, 128)
            here = slice(side * width, (side + 1) * width)
            if dim == 0:
                pair = src.at[0, pl.ds(start, width), :], part.at[here, :]
            else:
                pair = src.at[0, :, pl.ds(start, width)], part.at[:, here]
            copies.append(pltpu.make_async_copy(*pair, sem.at[n]))
    for copy in copies:
        copy.start()
    for copy in copies:
        copy.wait()


def fetch(weight, dim, at, *after):
    count = at.shape[0] // 2
    shape = list(weight.shape[1:])
    shape[dim] //= count
    weight = pltpu.with_memory_space_constraint(weight, pltpu.HBM)
    return pl.pallas_call(
        functools.partial(fetch_kernel, dim, count),
        in_specs=[pl.BlockSpec(memory_space=pltpu.SMEM)]
        + [pl.BlockSpec(memory_space=pl.ANY)] * (1 + len(after)),
        out_specs=[pl.BlockSpec(memory_space=pltpu.VMEM)] * count,
        out_shape=[pltpu.VMEM(tuple(shape), weight.dtype)] * count,
        scratch_shapes=[pltpu.SemaphoreType.DMA((2 * count,))],
        compiler_params=pltpu.CompilerParams(vmem_limit_bytes=1024 * 1024),
        cost_estimate=pl.CostEstimate(
            flops=0, bytes_accessed=2 * math.prod(weight.shape), transcendentals=0
        ),
        name="fetch",
    )(at, weight, *after)


def swap(value, axis, mask):
    size = lax.axis_size(axis)
    return lax.ppermute(value, axis, [(i, i ^ mask) for i in range(size)])


def dot(a, b):
    return jnp.dot(a, b, preferred_element_type=jnp.float32)


def share(value):
    chips = lax.axis_size("section") // 2
    return [value] + [swap(value, "section", 2 * k) for k in range(1, chips)]


def exchange(parts):
    count = lax.axis_size("expert")
    arrived = {k: swap(parts[k], "expert", k) for k in reversed(range(1, count))}
    return [arrived[k] for k in range(1, count)]


def per_device(
    resid,
    query,
    new_keys,
    new_values,
    cache_keys,
    cache_values,
    cache_len,
    out_weight,
    expert_ids,
    gates,
    w_gate,
    w_up,
    w_down,
):
    f32, bf16 = jnp.float32, jnp.bfloat16
    sections = lax.axis_size("section")
    experts = lax.axis_size("expert")
    chips = sections // 2
    section = lax.axis_index("section")
    own = lax.axis_index("expert")
    chip, core = section // 2, section % 2
    block_rows, width = resid.shape
    capacity = (block_rows * TOP * 5 + 4 * experts - 1) // (4 * experts)
    slots = -(-capacity // 16) * 16

    ids = lax.dynamic_slice_in_dim(expert_ids, own * block_rows, block_rows, 0)
    relative = ids ^ own
    order = jnp.arange(experts, dtype=jnp.int32)
    names = relative[:, :, None] == order
    named = jnp.any(names, axis=1)
    row = jnp.arange(block_rows, dtype=jnp.int32)
    earlier = (row[None, :] < row[:, None]).astype(bf16)
    rank = dot(earlier, named.astype(bf16)).astype(jnp.int32)
    slot = jnp.arange(slots, dtype=jnp.int32)
    hit = rank[:, :, None] == slot
    pick = (hit & named[:, :, None]).astype(bf16).reshape(block_rows, experts * slots)
    place = [
        (hit & names[:, k, :, None]).astype(bf16).reshape(block_rows, experts * slots)
        for k in range(TOP)
    ]

    attended, out_weight = attend(
        query, new_keys, new_values, cache_keys, cache_values, cache_len, out_weight
    )
    same = [attended] + [swap(attended, "section", 2 * k) for k in range(1, chips)]
    step = jnp.arange(2 * chips, dtype=jnp.int32)
    found = section ^ step
    block = (step % chips) ^ chip ^ own
    places = block * 2 + (core ^ (step // chips))
    found, places = lax.optimization_barrier((found, places))
    same, gate_parts = lax.optimization_barrier((same, fetch(w_gate, 0, found, attended)))
    other = [swap(v, "section", 1) for v in same]
    projected = list(project(places, same + other, out_weight, experts))
    arrived = exchange(projected)
    hidden, up_parts = lax.optimization_barrier(
        (resid.astype(f32) + projected[0], fetch(w_up, 0, found, projected[0]))
    )
    for part in arrived:
        hidden = hidden + part.astype(f32)
    hidden_in = hidden.astype(bf16)

    buffers = lax.dot_general(
        pick, hidden_in, (((0,), (0,)), ((), ())), preferred_element_type=f32
    ).astype(bf16)
    buffers = buffers.reshape(experts, slots, width)
    first = {k: swap(buffers[0], "section", 2 * k) for k in range(1, chips)}
    rest = jnp.concatenate(exchange(buffers), axis=0)
    rest, first = lax.optimization_barrier((rest, first))
    down_parts = fetch(w_down, 1, found, rest)
    received = jnp.concatenate([buffers[0], rest], axis=0)
    second = {k: swap(rest, "section", 2 * k) for k in range(1, chips)}

    sums = []
    for k in range(chips):
        if k:
            first[k], second[k], down_parts, sums = lax.optimization_barrier(
                (first[k], second[k], down_parts, sums)
            )
        same = jnp.concatenate([first[k], second[k]], axis=0) if k else received
        for side, piece in enumerate((same, swap(same, "section", 1))):
            here = slice(side * width, (side + 1) * width)
            parts = [dot(piece, w[k][here]) for w in (gate_parts, up_parts)]
            sums = [a + b for a, b in zip(sums, parts)] if sums else parts
    gate_acc, up_acc = sums
    activated = (jax.nn.silu(gate_acc) * up_acc).astype(bf16)

    def down(k, side):
        here = slice(side * width, (side + 1) * width)
        return dot(activated, down_parts[k][:, here])

    order = sorted(range(1, chips), key=lambda k: (-(k & 2), -k))
    ahead = {k: down(k, 1).astype(bf16) for k in order if k & 2}
    later, rest = {}, {}
    for k in order:
        for_core = ahead[k] if k in ahead else down(k, 1).astype(bf16)
        both = (down(k, 0) + swap(for_core, "section", 1).astype(f32)).astype(bf16)
        later[k], rest[k] = both[:slots], both[slots:]
        if k in ahead:
            later[k], rest[k], activated = lax.optimization_barrier((later[k], rest[k], activated))
    rest = {k: swap(rest[k], "section", 2 * k) for k in order}
    total = down(0, 0) + swap(down(0, 1).astype(bf16), "section", 1).astype(f32)
    mine, total = total[:slots], total[slots:]
    for k in order:
        total = total + rest[k].astype(f32)
    total, later = lax.optimization_barrier((total.astype(bf16), later))

    arrived = exchange([None] + jnp.split(total, experts - 1, axis=0))
    later = [swap(later[k], "section", 2 * k) for k in order]
    mine, arrived = lax.optimization_barrier((mine, arrived))
    for part in later:
        mine = mine + part.astype(f32)
    returned = jnp.concatenate([mine.astype(bf16)] + arrived, axis=0)
    mixture = sum(gates[:, k : k + 1] * dot(place[k], returned) for k in range(TOP))
    return (hidden_in.astype(f32) + mixture).astype(bf16)


def solution(mesh):
    in_specs = (
        P("expert", "section"),
        P("section", "expert"),
        P("section", "expert"),
        P("section", "expert"),
        P("section", None, "expert"),
        P("section", None, "expert"),
        P("section"),
        P("expert", "section"),
        P(),
        P("expert", None),
        P("expert", None, "section"),
        P("expert", None, "section"),
        P("expert", "section", None),
    )
    out_specs = P("expert", "section")
    return jax.shard_map(
        per_device, mesh=mesh, in_specs=in_specs, out_specs=out_specs, check_vma=False
    )
```

```python
import functools
import math

import jax
import jax.numpy as jnp
from jax import lax
from jax.experimental import pallas as pl
from jax.experimental.pallas import tpu as pltpu
from jax.sharding import PartitionSpec as P

HQ = 48
KV = 8
HD = 128
TOP = 2
GROUPS = HQ // KV
SCALE = 1.0 / math.sqrt(HD)
MASKED = -1e30
NT = (((1,), (1,)), ((), ()))


def spread(rows, drafts, transposed):
    shape = (rows, rows // drafts * 8) if transposed else (rows // drafts * 8, rows)
    at = lax.broadcasted_iota(jnp.int32, shape, 1 if transposed else 0)
    row = lax.broadcasted_iota(jnp.int32, shape, 0 if transposed else 1)
    inside = at & 7
    return ((inside < drafts) & ((at >> 3) * drafts + inside == row)).astype(jnp.bfloat16)


def attend_kernel(
    drafts, len_hbm, q_hbm, nk_hbm, nv_hbm, ck_hbm, cv_hbm, w_hbm, o_ref, w_ref, *scratch
):
    len_ref, q_ref, nk_ref, nv_ref, ck_ref, cv_ref, *scratch = scratch
    qs, spread_q, scores, new_scores, new_probs, mixed, inverse, acc, *scratch = scratch
    sem, k_sem, v_sem, w_sem = scratch
    requests, size, width = ck_ref.shape
    rows = q_ref.shape[0]
    heads = width // HD
    group = GROUPS * 8
    wide = heads * group

    small = [
        pltpu.make_async_copy(src, dst, sem.at[i])
        for i, (src, dst) in enumerate(
            ((q_hbm, q_ref), (len_hbm, len_ref), (nk_hbm, nk_ref), (nv_hbm, nv_ref))
        )
    ]
    keys = [pltpu.make_async_copy(ck_hbm.at[r], ck_ref.at[r], k_sem.at[r]) for r in range(requests)]
    values = [
        pltpu.make_async_copy(cv_hbm.at[r], cv_ref.at[r], v_sem.at[r]) for r in range(requests)
    ]
    part = w_ref.shape[0] // 4
    weights = [
        pltpu.make_async_copy(
            w_hbm.at[i * part : (i + 1) * part], w_ref.at[i * part : (i + 1) * part], w_sem.at[i]
        )
        for i in range(4)
    ]
    for copy in small:
        copy.start()
    for pair in zip(keys, values):
        for copy in pair:
            copy.start()
    for copy in weights:
        copy.start()
    for copy in small:
        copy.wait()
    qs[...] = dot(spread(rows, drafts, False), q_ref[...])

    place = lax.broadcasted_iota(jnp.int32, (1, size), 1)
    for r in range(requests):
        q_all = qs[r * 8 : (r + 1) * 8, :]
        zero = jnp.zeros((group, HD), jnp.float32)
        parts = []
        for h in range(heads):
            q = jnp.concatenate(
                [
                    q_all[:, (h * GROUPS + g) * HD : (h * GROUPS + g + 1) * HD]
                    for g in range(GROUPS)
                ],
                axis=0,
            )
            parts.append(jnp.concatenate([q if j == h else zero for j in range(heads)], axis=1))
        spread_q[r * wide : (r + 1) * wide, :] = jnp.concatenate(parts, axis=0).astype(jnp.bfloat16)
    new_scores[...] = lax.dot_general(
        spread_q[...], nk_ref[...], NT, preferred_element_type=jnp.float32
    )
    at = lax.broadcasted_iota(jnp.int32, (wide, rows), 1)
    draft_at = lax.broadcasted_iota(jnp.int32, (wide, rows), 0) & 7

    def score(r):
        here = slice(r * wide, (r + 1) * wide)
        past = lax.dot_general(spread_q[here, :], ck_ref[r], NT, preferred_element_type=jnp.float32)
        scores[r % 4] = past * SCALE + jnp.where(place < len_ref[r], 0.0, MASKED)

    def mix(r):
        here = slice(r * wide, (r + 1) * wide)
        past = scores[r % 4]
        key_at = at - r * drafts
        new_ok = (key_at >= 0) & (key_at <= draft_at) & (key_at < drafts)
        new = jnp.where(new_ok, new_scores[here, :] * SCALE, MASKED)
        top = jnp.maximum(
            jnp.max(past, axis=1, keepdims=True), jnp.max(new, axis=1, keepdims=True)
        )
        past = jnp.exp(past - top)
        new = jnp.exp(new - top)
        total = jnp.sum(past, axis=1, keepdims=True) + jnp.sum(new, axis=1, keepdims=True)
        inverse[here, :] = jnp.broadcast_to(1.0 / total, (wide, HD))
        new_probs[here, :] = new.astype(jnp.bfloat16)
        mixed[here, :] = dot(past.astype(jnp.bfloat16), cv_ref[r])

    pairs = [range(i, min(i + 2, requests)) for i in range(0, requests, 2)]
    for r in pairs[0]:
        keys[r].wait()
    for r in pairs[0]:
        score(r)
    for i, pair in enumerate(pairs):
        following = pairs[i + 1] if i + 1 < len(pairs) else ()
        for r in following:
            keys[r].wait()
        for r in pair:
            values[r].wait()
        for r in following:
            score(r)
        for r in pair:
            mix(r)
    mixed[...] = mixed[...] + dot(new_probs[...], nv_ref[...])
    for r in range(requests):
        for h in range(heads):
            for g in range(GROUPS):
                col = (h * GROUPS + g) * HD
                row = slice(r * wide + h * group + g * 8, r * wide + h * group + (g + 1) * 8)
                acc[r * 8 : (r + 1) * 8, col : col + HD] = (
                    mixed[row, h * HD : (h + 1) * HD] * inverse[row, :]
                )
    kept = spread(rows, drafts, True)
    o_ref[...] = dot(kept, acc[...].astype(jnp.bfloat16)).astype(jnp.bfloat16)
    for copy in weights:
        copy.wait()


def attend(query, new_keys, new_values, cache_keys, cache_values, cache_len, weight):
    requests, size, width = cache_keys.shape
    rows, q_width = query.shape
    wide = width // HD * GROUPS * 8
    f32, bf16 = jnp.float32, jnp.bfloat16
    operands = [
        pltpu.with_memory_space_constraint(v, pltpu.HBM)
        for v in (cache_len, query, new_keys, new_values, cache_keys, cache_values, weight)
    ]
    return pl.pallas_call(
        functools.partial(attend_kernel, rows // requests),
        in_specs=[pl.BlockSpec(memory_space=pl.ANY)] * len(operands),
        out_specs=[pl.BlockSpec(memory_space=pltpu.VMEM)] * 2,
        out_shape=[
            jax.ShapeDtypeStruct(query.shape, bf16),
            pltpu.VMEM(weight.shape, weight.dtype),
        ],
        scratch_shapes=[
            pltpu.SMEM(cache_len.shape, jnp.int32),
            pltpu.VMEM(query.shape, bf16),
            pltpu.VMEM(new_keys.shape, bf16),
            pltpu.VMEM(new_values.shape, bf16),
            pltpu.VMEM(cache_keys.shape, bf16),
            pltpu.VMEM(cache_values.shape, bf16),
            pltpu.VMEM((requests * 8, q_width), f32),
            pltpu.VMEM((requests * wide, width), bf16),
            pltpu.VMEM((4, wide, size), f32),
            pltpu.VMEM((requests * wide, rows), f32),
            pltpu.VMEM((requests * wide, rows), bf16),
            pltpu.VMEM((requests * wide, width), f32),
            pltpu.VMEM((requests * wide, HD), f32),
            pltpu.VMEM((requests * 8, q_width), f32),
            pltpu.SemaphoreType.DMA((4,)),
            pltpu.SemaphoreType.DMA((requests,)),
            pltpu.SemaphoreType.DMA((requests,)),
            pltpu.SemaphoreType.DMA((4,)),
        ],
        compiler_params=pltpu.CompilerParams(vmem_limit_bytes=20 * 1024 * 1024),
        cost_estimate=pl.CostEstimate(
            flops=4 * rows * size * q_width,
            bytes_accessed=4 * requests * size * width,
            transcendentals=rows * size * q_width // HD,
        ),
        name="attend",
    )(*operands)


def project_kernel(at_ref, *refs):
    pieces, (w_ref, own_ref, *out_refs, scratch) = refs[: at_ref.shape[0]], refs[at_ref.shape[0] :]
    part = pieces[0].shape[0]
    rows = own_ref.shape[0]
    for i, piece in enumerate(pieces):
        scratch[pl.ds(pl.multiple_of(at_ref[i] * part, 16), part), :] = piece[...]
    product = dot(scratch[...], w_ref[...])
    own_ref[...] = product[:rows, :]
    for i, out in enumerate(out_refs):
        out[...] = product[(i + 1) * rows : (i + 2) * rows, :].astype(out.dtype)


def project(places, pieces, weight, blocks):
    part, depth = pieces[0].shape
    width = weight.shape[1]
    rows = part * len(pieces) // blocks
    vmem = pl.BlockSpec(memory_space=pltpu.VMEM)
    own = jax.ShapeDtypeStruct((rows, width), jnp.float32)
    sent = jax.ShapeDtypeStruct((rows, width), jnp.bfloat16)
    return pl.pallas_call(
        project_kernel,
        in_specs=[pl.BlockSpec(memory_space=pltpu.SMEM)] + [vmem] * (len(pieces) + 1),
        out_specs=[vmem] * blocks,
        out_shape=[own] + [sent] * (blocks - 1),
        scratch_shapes=[pltpu.VMEM((part * len(pieces), depth), jnp.bfloat16)],
        compiler_params=pltpu.CompilerParams(vmem_limit_bytes=8 * 1024 * 1024),
        cost_estimate=pl.CostEstimate(
            flops=2 * part * len(pieces) * depth * width,
            bytes_accessed=2 * depth * width,
            transcendentals=0,
        ),
        name="project",
    )(places, *pieces, weight)


def fetch_kernel(dim, count, at_ref, src, *refs):
    parts, sem = refs[-1 - count : -1], refs[-1]
    width = parts[0].shape[dim] // 2
    copies = []
    for i, part in enumerate(parts):
        for side in range(2):
            n = 2 * i + side
            start = pl.multiple_of(at_ref[n] * width, 128)
            here = slice(side * width, (side + 1) * width)
            if dim == 0:
                pair = src.at[0, pl.ds(start, width), :], part.at[here, :]
            else:
                pair = src.at[0, :, pl.ds(start, width)], part.at[:, here]
            copies.append(pltpu.make_async_copy(*pair, sem.at[n]))
    for copy in copies:
        copy.start()
    for copy in copies:
        copy.wait()


def fetch(weight, dim, at, *after):
    count = at.shape[0] // 2
    shape = list(weight.shape[1:])
    shape[dim] //= count
    weight = pltpu.with_memory_space_constraint(weight, pltpu.HBM)
    return pl.pallas_call(
        functools.partial(fetch_kernel, dim, count),
        in_specs=[pl.BlockSpec(memory_space=pltpu.SMEM)]
        + [pl.BlockSpec(memory_space=pl.ANY)] * (1 + len(after)),
        out_specs=[pl.BlockSpec(memory_space=pltpu.VMEM)] * count,
        out_shape=[pltpu.VMEM(tuple(shape), weight.dtype)] * count,
        scratch_shapes=[pltpu.SemaphoreType.DMA((2 * count,))],
        compiler_params=pltpu.CompilerParams(vmem_limit_bytes=1024 * 1024),
        cost_estimate=pl.CostEstimate(
            flops=0, bytes_accessed=2 * math.prod(weight.shape), transcendentals=0
        ),
        name="fetch",
    )(at, weight, *after)


def swap(value, axis, mask):
    size = lax.axis_size(axis)
    return lax.ppermute(value, axis, [(i, i ^ mask) for i in range(size)])


def dot(a, b):
    return jnp.dot(a, b, preferred_element_type=jnp.float32)


def share(value):
    chips = lax.axis_size("section") // 2
    return [value] + [swap(value, "section", 2 * k) for k in range(1, chips)]


def exchange(parts):
    count = lax.axis_size("expert")
    arrived = {k: swap(parts[k], "expert", k) for k in reversed(range(1, count))}
    return [arrived[k] for k in range(1, count)]


def per_device(
    resid,
    query,
    new_keys,
    new_values,
    cache_keys,
    cache_values,
    cache_len,
    out_weight,
    expert_ids,
    gates,
    w_gate,
    w_up,
    w_down,
):
    f32, bf16 = jnp.float32, jnp.bfloat16
    sections = lax.axis_size("section")
    experts = lax.axis_size("expert")
    chips = sections // 2
    section = lax.axis_index("section")
    own = lax.axis_index("expert")
    chip, core = section // 2, section % 2
    block_rows, width = resid.shape
    capacity = (block_rows * TOP * 5 + 4 * experts - 1) // (4 * experts)
    slots = -(-capacity // 16) * 16

    ids = lax.dynamic_slice_in_dim(expert_ids, own * block_rows, block_rows, 0)
    relative = ids ^ own
    order = jnp.arange(experts, dtype=jnp.int32)
    names = relative[:, :, None] == order
    named = jnp.any(names, axis=1)
    row = jnp.arange(block_rows, dtype=jnp.int32)
    earlier = (row[None, :] < row[:, None]).astype(bf16)
    rank = dot(earlier, named.astype(bf16)).astype(jnp.int32)
    slot = jnp.arange(slots, dtype=jnp.int32)
    hit = rank[:, :, None] == slot
    pick = (hit & named[:, :, None]).astype(bf16).reshape(block_rows, experts * slots)
    place = [
        (hit & names[:, k, :, None]).astype(bf16).reshape(block_rows, experts * slots)
        for k in range(TOP)
    ]

    attended, out_weight = attend(
        query, new_keys, new_values, cache_keys, cache_values, cache_len, out_weight
    )
    same = [attended] + [swap(attended, "section", 2 * k) for k in range(1, chips)]
    step = jnp.arange(2 * chips, dtype=jnp.int32)
    found = section ^ step
    block = (step % chips) ^ chip ^ own
    places = block * 2 + (core ^ (step // chips))
    found, places = lax.optimization_barrier((found, places))
    same, gate_parts = lax.optimization_barrier((same, fetch(w_gate, 0, found, attended)))
    other = [swap(v, "section", 1) for v in same]
    projected = list(project(places, same + other, out_weight, experts))
    arrived = exchange(projected)
    hidden, up_parts = lax.optimization_barrier(
        (resid.astype(f32) + projected[0], fetch(w_up, 0, found, projected[0]))
    )
    for part in arrived:
        hidden = hidden + part.astype(f32)
    hidden_in = hidden.astype(bf16)

    buffers = lax.dot_general(
        pick, hidden_in, (((0,), (0,)), ((), ())), preferred_element_type=f32
    ).astype(bf16)
    buffers = buffers.reshape(experts, slots, width)
    half = experts // 2
    arrived = {0: buffers[0]}
    for k in [*range(1, half), *reversed(range(half, experts))]:
        arrived[k] = swap(buffers[k], "expert", k)
    near = jnp.concatenate([arrived[k] for k in range(half)], axis=0)
    first = {k: swap(near, "section", 2 * k) for k in range(1, chips)}
    rest = jnp.concatenate([arrived[k] for k in range(half, experts)], axis=0)
    rest, first, down_parts = lax.optimization_barrier(
        (rest, first, fetch(w_down, 1, found, near))
    )
    received = jnp.concatenate([near, rest], axis=0)
    second = {k: swap(rest, "section", 2 * k) for k in range(1, chips)}

    sums = []
    for k in range(chips):
        if k:
            first[k], second[k], down_parts, sums = lax.optimization_barrier(
                (first[k], second[k], down_parts, sums)
            )
        same = jnp.concatenate([first[k], second[k]], axis=0) if k else received
        for side, piece in enumerate((same, swap(same, "section", 1))):
            here = slice(side * width, (side + 1) * width)
            parts = [dot(piece, w[k][here]) for w in (gate_parts, up_parts)]
            sums = [a + b for a, b in zip(sums, parts)] if sums else parts
    gate_acc, up_acc = sums
    activated = (jax.nn.silu(gate_acc) * up_acc).astype(bf16)

    def down(k, side):
        here = slice(side * width, (side + 1) * width)
        return dot(activated, down_parts[k][:, here])

    order = sorted(range(1, chips), key=lambda k: (-(k & 2), -k))
    ahead = {k: down(k, 1).astype(bf16) for k in order if k & 2}
    later, rest = {}, {}
    for k in order:
        for_core = ahead[k] if k in ahead else down(k, 1).astype(bf16)
        both = (down(k, 0) + swap(for_core, "section", 1).astype(f32)).astype(bf16)
        later[k], rest[k] = both[:slots], both[slots:]
        if k in ahead:
            later[k], rest[k], activated = lax.optimization_barrier((later[k], rest[k], activated))
    rest = {k: swap(rest[k], "section", 2 * k) for k in order}
    total = down(0, 0) + swap(down(0, 1).astype(bf16), "section", 1).astype(f32)
    mine, total = total[:slots], total[slots:]
    for k in order:
        total = total + rest[k].astype(f32)
    total, later = lax.optimization_barrier((total.astype(bf16), later))

    arrived = exchange([None] + jnp.split(total, experts - 1, axis=0))
    later = [swap(later[k], "section", 2 * k) for k in order]
    mine, arrived = lax.optimization_barrier((mine, arrived))
    for part in later:
        mine = mine + part.astype(f32)
    returned = jnp.concatenate([mine.astype(bf16)] + arrived, axis=0)
    mixture = sum(gates[:, k : k + 1] * dot(place[k], returned) for k in range(TOP))
    return (hidden_in.astype(f32) + mixture).astype(bf16)


def solution(mesh):
    in_specs = (
        P("expert", "section"),
        P("section", "expert"),
        P("section", "expert"),
        P("section", "expert"),
        P("section", None, "expert"),
        P("section", None, "expert"),
        P("section"),
        P("expert", "section"),
        P(),
        P("expert", None),
        P("expert", None, "section"),
        P("expert", None, "section"),
        P("expert", "section", None),
    )
    out_specs = P("expert", "section")
    return jax.shard_map(
        per_device, mesh=mesh, in_specs=in_specs, out_specs=out_specs, check_vma=False
    )
```
